32 devices in a mesh: dp: 2 (over core), ctx: 8 (over z, y), tp: 2 (over x).
Axes of the slice: x: 2, y: 2, z: 4, core: 2. Of those that a mesh axis runs over, the one named last changes fastest.
Arguments:
- teacher_part: bfloat16 [2, 2, 2048, 8192], P('dp', 'tp', 'ctx'), may hold values from -8 to 8
- student_in: bfloat16 [2, 2048, 4096], P('dp', 'ctx'), may hold values from -24 to 24
- out_proj: bfloat16 [4096, 4096], P('ctx', 'tp'), may hold values from -0.09375 to 0.09375
- segment_ids: int32 [2, 2048], P('dp'), may hold values from 0 to 3, never falling along the last dimension, each value on 1 to 1024 neighbouring positions
- valid_count: int32 [2], P('dp'), may hold values from 256 to 2048, as said below
Outputs:
- doc_loss: float32 [2], P('dp')
- wo_grad: float32 [4096, 4096], P('ctx', 'tp')
- state_grad: float32 [2, 2048, 4096], P('dp', 'ctx', 'tp')
The draws below stay inside these ranges and needn't reach their ends.
Inputs may be any that keep to these rules, and one draw needn't show every extreme that they name: `valid_count`: one document in every draw is valid at all 2048 positions. `segment_ids`: segment numbers never fall along a document.
All inputs are finite; a program needn't handle non-finite values.
Results may differ from the reference program's by a relative error of at most 0.019.
The reference program's roundings to bfloat16 on the way (of `teacher_hidden`, `student_hidden`, `score_grad` and `hidden_grad`) count: a program that leaves them out, or rounds other values in their place, can miss the bound.
Values may be sent and summed in bfloat16 or wider, within the bound.
No kernel may reach another device: no remote copies, remote signals or barrier semaphores. Data moves between devices by JAX's collectives and lax.ppermute only.
A program may use at most 64 MiB of HBM per device.

```python
import math
import jax
import jax.numpy as jnp
import numpy as np
from jax import lax

DT = 8192
DS = 4096
HEADS = 32
TOK_DEV = 256
SEQ = 2048
DOCS = 2
SEGS = 4
SEG_MOST = 1024
N_CTX = 8
N_TP = 2


def draw_teacher_part(key, part):
    key_base, key_scale = jax.random.split(key, 2)
    shape = (DOCS, N_TP, SEQ, DT)
    base = jnp.clip(jax.random.normal(key_base, shape, jnp.float32), -5.0, 5.0)
    row_scale = jnp.exp(jax.random.uniform(key_scale, (DOCS, 1, SEQ, 1), jnp.float32, math.log(0.4), math.log(4.0)))
    return (0.25 * base * row_scale).astype(jnp.bfloat16)


def draw_student_input(key, part):
    key_base, key_scale = jax.random.split(key, 2)
    shape = (DOCS, SEQ, DS)
    base = jnp.clip(jax.random.normal(key_base, shape, jnp.float32), -5.0, 5.0)
    row_scale = jnp.exp(jax.random.uniform(key_scale, (DOCS, SEQ, 1), jnp.float32, math.log(0.4), math.log(4.0)))
    return base * row_scale


def draw_student_in(key, part):
    return draw_student_input(key, part).astype(jnp.bfloat16)


def draw_valid_count(key, part):
    key_count, key_full = jax.random.split(key, 2)
    counts = jax.random.randint(key_count, (DOCS,), TOK_DEV, SEQ + 1)
    full_doc = jax.random.randint(key_full, (), 0, DOCS)
    return jnp.where(jnp.arange(DOCS, dtype=jnp.int32) == full_doc, SEQ, counts).astype(jnp.int32)


def levels(rng, extent, cuts, smallest, largest):
    factor_of, own = 1.0, jax.random.fold_in(rng, 6)
    for dim, shards_of in cuts:
        heights = jnp.exp(jax.random.uniform(jax.random.fold_in(own, dim), (shards_of,), jnp.float32, smallest / len(cuts), largest / len(cuts)))
        factor_of = factor_of * jnp.repeat(heights, extent[dim] // shards_of).reshape([-1 if axis == dim else 1 for axis in range(len(extent))])
    return factor_of


def split_up(count, total, limit, slope):
    portions = [(1 << 20) // math.isqrt(grade ** slope) + 1 for grade in range(2, count + 1)]
    spare, given = total - limit - (count - 1), [1] * (count - 1)
    while spare > 0:
        candidates = [i for i in range(count - 1) if given[i] < limit]
        whole, left = sum([portions[i] for i in candidates]), spare
        for i in candidates:
            more = min(limit - given[i], max(1, left * portions[i] // whole), spare)
            given[i] = given[i] + more
            spare = spare - more
    return np.array([limit] + given)


def ragged_sizes(key, amount, total, reach, skew):
    if amount == 2:
        one = jax.random.randint(key, (), max(1, total - reach), min(reach, total - 1) + 1)
        return jnp.stack([one, total - one])
    lengths = jnp.asarray(split_up(amount, total, reach, skew), jnp.int32)
    pairs = (amount - 1) // 2
    donor, taker = lengths[1:1 + 2 * pairs:2], lengths[2:2 + 2 * pairs:2]
    margin = jnp.minimum(donor - 1, reach - taker)
    passed = jax.random.randint(jax.random.fold_in(key, 1), (pairs,), 0, 1 << 20) % (margin + 1)
    lengths = lengths.at[1:1 + 2 * pairs:2].set(donor - passed).at[2:2 + 2 * pairs:2].set(taker + passed)
    return lengths[jax.random.permutation(jax.random.fold_in(key, 2), amount)]


def bell_draw(own_key, dims, scale, bound, cuts=(), kind=jnp.bfloat16):
    gain = levels(own_key, dims, cuts, -0.22, 0.18) if cuts else 1.0
    entries = jax.random.normal(own_key, dims, jnp.float32) * scale * gain
    return jnp.minimum(jnp.maximum(entries, -bound), bound).astype(kind)


def setup_inputs(seed: int = 0) -> dict:
    splits = jax.random.split(jax.random.key(seed), 6)
    teacher_part = draw_teacher_part(jax.random.fold_in(splits[5], 71), 0)
    student_in = draw_student_in(jax.random.fold_in(splits[5], 71), 0)
    out_proj = bell_draw(splits[2], (DS, DS), DS ** -0.5, 0.09375, ((0, 8), (1, 2)))
    segment_ids = jax.vmap(lambda own: jnp.searchsorted(jnp.cumsum(ragged_sizes(own, SEGS, SEQ, SEG_MOST, 1)), jnp.arange(SEQ), side="right"))(jax.random.split(splits[3], DOCS)).reshape((DOCS, SEQ)).astype(jnp.int32)
    valid_count = draw_valid_count(jax.random.fold_in(splits[5], 71), 0)
    return {"teacher_part": teacher_part, "student_in": student_in, "out_proj": out_proj, "segment_ids": segment_ids, "valid_count": valid_count}


masked_score = -1e+30

def log_probs(scores, allowed):
    scores = jnp.where(allowed[None, :, :], scores, masked_score)
    top = lax.optimization_barrier(jnp.max(scores, axis=-1, keepdims=True))
    shifted = scores - top
    return shifted - jnp.log(lax.optimization_barrier(jnp.sum(jnp.exp(shifted), axis=-1, keepdims=True)))

def window_terms(teacher_query, teacher_keys, student_query, student_keys, allowed, live):
    length = teacher_query.shape[0]
    teacher_qh = teacher_query.reshape(length, HEADS, -1).astype(jnp.float32)
    teacher_kh = teacher_keys.reshape(2 * length, HEADS, -1).astype(jnp.float32)
    student_qh = student_query.reshape(length, HEADS, -1).astype(jnp.float32)
    student_kh = student_keys.reshape(2 * length, HEADS, -1).astype(jnp.float32)
    teacher_scale = 1.0 / math.sqrt(teacher_qh.shape[-1])
    student_scale = 1.0 / math.sqrt(student_qh.shape[-1])
    teacher_scores = jnp.einsum('qhd,khd->hqk', teacher_qh, teacher_kh, precision=lax.Precision.HIGHEST) * teacher_scale
    student_scores = jnp.einsum('qhd,khd->hqk', student_qh, student_kh, precision=lax.Precision.HIGHEST) * student_scale
    teacher_logp = log_probs(teacher_scores, allowed)
    student_logp = log_probs(student_scores, allowed)
    teacher_prob = jnp.exp(teacher_logp)
    student_prob = jnp.exp(student_logp)
    divergence = lax.optimization_barrier(jnp.sum(teacher_prob * (teacher_logp - student_logp), axis=-1))
    loss_part = jnp.sum(divergence * live[None, :]) / HEADS
    grad_scale = live[None, :, None] * (student_scale / HEADS)
    score_grad = ((student_prob - teacher_prob) * grad_scale).astype(jnp.bfloat16).astype(jnp.float32)
    query_grad = jnp.einsum('hqk,khd->qhd', score_grad, student_kh, precision=lax.Precision.HIGHEST).reshape(length, -1)
    key_grad = jnp.einsum('hqk,qhd->khd', score_grad, student_qh, precision=lax.Precision.HIGHEST).reshape(2 * length, -1)
    return (loss_part, query_grad, key_grad)

def reference(teacher_part, student_in, out_proj, segment_ids, valid_count):
    unscale = HEADS * math.sqrt(DS // HEADS)

    def document_terms(index):
        teacher_doc = teacher_part[index]
        student_doc = student_in[index]
        segments = segment_ids[index]
        valid_limit = valid_count[index]
        teacher_hidden = lax.optimization_barrier(jnp.sum(teacher_doc.astype(jnp.float32), axis=0)).astype(jnp.bfloat16)
        student_hidden = jnp.dot(student_doc, out_proj, preferred_element_type=jnp.float32).astype(jnp.bfloat16)
        teacher_padded = jnp.concatenate([jnp.zeros((TOK_DEV, DT), jnp.bfloat16), teacher_hidden], 0)
        student_padded = jnp.concatenate([jnp.zeros((TOK_DEV, DS), jnp.bfloat16), student_hidden], 0)
        segment_padded = jnp.concatenate([jnp.full((TOK_DEV,), -1, jnp.int32), segments.astype(jnp.int32)], 0)

        def one_window(window):
            start = (window * TOK_DEV).astype(jnp.int32)
            teacher_query = lax.dynamic_slice_in_dim(teacher_hidden, start, TOK_DEV, 0)
            teacher_keys = lax.dynamic_slice_in_dim(teacher_padded, start, 2 * TOK_DEV, 0)
            student_query = lax.dynamic_slice_in_dim(student_hidden, start, TOK_DEV, 0)
            student_keys = lax.dynamic_slice_in_dim(student_padded, start, 2 * TOK_DEV, 0)
            query_segment = lax.dynamic_slice_in_dim(segments.astype(jnp.int32), start, TOK_DEV, 0)
            key_segment = lax.dynamic_slice_in_dim(segment_padded, start, 2 * TOK_DEV, 0)
            query_position = start + jnp.arange(TOK_DEV, dtype=jnp.int32)
            key_position = start - TOK_DEV + jnp.arange(2 * TOK_DEV, dtype=jnp.int32)
            allowed = (key_segment[None, :] == query_segment[:, None]) & (key_position[None, :] < valid_limit)
            live = jnp.where(query_position < valid_limit, 1.0, 0.0).astype(jnp.float32)
            return window_terms(teacher_query, teacher_keys, student_query, student_keys, allowed, live)
        losses, query_grads, key_grads = lax.map(one_window, jnp.arange(N_CTX, dtype=jnp.int32))
        own_grad = query_grads + key_grads[:, TOK_DEV:]
        from_next = jnp.concatenate([key_grads[1:, :TOK_DEV], jnp.zeros((1, TOK_DEV, DS), jnp.float32)], 0)
        hidden_grad = (own_grad + from_next).reshape(SEQ, DS).astype(jnp.bfloat16)
        doc_grad = jnp.dot(student_doc.T, hidden_grad, preferred_element_type=jnp.float32)
        scaled = hidden_grad.astype(jnp.float32) * unscale
        return (jnp.sum(losses), doc_grad, scaled)
    doc_loss, doc_grads, state_grad = lax.map(document_terms, jnp.arange(DOCS, dtype=jnp.int32))
    return (doc_loss, lax.optimization_barrier(jnp.sum(doc_grads, axis=0)), state_grad)
```

```python
import functools
import math

import jax
import jax.numpy as jnp
from jax import lax
from jax.experimental import pallas as pl
from jax.experimental.layout import Layout, with_layout_constraint
from jax.experimental.pallas import tpu as pltpu
from jax.sharding import PartitionSpec as P

DS = 4096
HEADS = 32
CHUNKS = 2
HEADS_A_STEP = 2
MASKED = -1e30


def after(value, *earlier):
    return lax.optimization_barrier((value, *earlier))[0]


def row_major(value):
    return with_layout_constraint(value, Layout(tuple(range(value.ndim))))


def rotate(value, axis, steps):
    count = lax.axis_size(axis)
    return lax.ppermute(value, axis, [(i, (i + steps) % count) for i in range(count)])


def swap(value, axis, distance):
    count = lax.axis_size(axis)
    return lax.ppermute(value, axis, [(i, i ^ distance) for i in range(count)])


def shift(value, axis, steps):
    count = lax.axis_size(axis)
    pairs = [(i, i + steps) for i in range(count) if 0 <= i + steps < count]
    return lax.ppermute(value, axis, pairs)


def ordered(mine, other, place):
    first = lax.select(place == 0, mine, other)
    second = lax.select(place == 0, other, mine)
    return first, second


def send_line(value, axis, upward=(), downward=()):
    pairs = [(2 * i + j, 2 * i + 2 + j) for i in upward for j in range(2)]
    pairs += [(2 * i + j, 2 * i - 2 + j) for i in downward for j in range(2)]
    return lax.ppermute(value, axis, pairs)


def gather_line(block, axis, gates):
    groups, group = lax.axis_size(axis) // 2, lax.axis_index(axis) >> 1
    out, up, down, either = [(group, block)], block, block, None
    for hop in range(1, groups):
        upward, downward = range(hop - 1, groups - 1), range(1, groups - hop + 1)
        gate = gates.get(hop, ())
        below, above = jnp.maximum(group - hop, 0), jnp.minimum(group + hop, groups - 1)
        if either is None:
            if gate:
                up, down = after(up, *gate), after(down, *gate)
            up = send_line(up, axis, upward=upward)
            down = send_line(down, axis, downward=downward)
            if 2 * hop < groups:
                out += [(below, up), (above, down)]
                continue
            either = lax.select(group >= hop, up, down)
        else:
            if gate:
                either = after(either, *gate)
            either = send_line(either, axis, upward, downward)
        out.append((lax.select(group >= hop, below, above), either))
    return out


def scatter_line(blocks, axis):
    groups, group = lax.axis_size(axis) // 2, lax.axis_index(axis) >> 1

    def plus(target, came):
        block = lax.dynamic_index_in_dim(blocks, target, 0, keepdims=False)
        return block if came is None else block + came.astype(jnp.float32)

    up = down = None
    for step in range(1, groups):
        upward, downward = range(min(step, groups - 1)), range(max(groups - step, 1), groups)
        rising = plus(jnp.minimum(groups - step + group, groups - 1), up).astype(jnp.bfloat16)
        falling = plus(jnp.maximum(group + step - groups, 0), down).astype(jnp.bfloat16)
        if 2 * step < groups - 1:
            value = lax.select(group < step, rising, falling)
            came = send_line(value, axis, upward, downward)
            none = jnp.zeros_like(came)
            up = lax.select(group <= step, came, none)
            down = lax.select(group >= groups - 1 - step, came, none)
        else:
            up = send_line(rising, axis, upward=upward)
            down = send_line(falling, axis, downward=downward)
    return plus(group, up) + down.astype(jnp.float32), (up, down)


def by_owner(parts, me):
    count = len(parts)
    if count == 2:
        return ordered(*parts, me)
    parts = jnp.stack(parts)
    return [
        lax.dynamic_index_in_dim(parts, lax.rem(me + count - i, count), 0, keepdims=False)
        for i in range(count)
    ]


def split_kernel(count, rows, tokens, out):
    width = tokens.shape[1] // count // rows
    for piece in range(count):
        for row in range(rows):
            start = (row * count + piece) * width
            out[piece, :, row * width : (row + 1) * width] = tokens[:, start : start + width]


def split(tokens, blocks, count):
    length, width = tokens.shape
    rows = max(1, 128 * blocks * count // width)
    step = width // blocks * rows
    return pl.pallas_call(
        functools.partial(split_kernel, count, rows),
        grid=(blocks // rows,),
        in_specs=[pl.BlockSpec((length, step), lambda i: (0, i))],
        out_specs=pl.BlockSpec((count, length, step // count), lambda i: (0, 0, i)),
        out_shape=jax.ShapeDtypeStruct((count, length, width // count), tokens.dtype),
        compiler_params=pltpu.CompilerParams(vmem_limit_bytes=16 * 1024 * 1024),
        cost_estimate=pl.CostEstimate(
            flops=0, bytes_accessed=4 * length * width, transcendentals=0
        ),
        name="split_tokens",
    )(tokens)


def attention_kernel(teacher_scale, student_scale, grad_scale, heads, *refs):
    teacher, student = refs[0:3], refs[3:6]
    bias, live, loss = refs[6], refs[7], refs[8]
    grad_past, grad_first, grad_second = refs[9:12]
    length = student[0].shape[0]
    dt, ds = teacher[0].shape[1] // heads, student[0].shape[1] // heads
    log2e = math.log2(math.e)

    @pl.when(pl.program_id(0) == 0)
    def _():
        loss[...] = jnp.zeros_like(loss)

    def scores(keys, queries, scale, mask):
        product = lax.dot_general(
            keys, queries, (((1,), (1,)), ((), ())), preferred_element_type=jnp.float32
        )
        return product * (scale * log2e) + mask

    def soft(first, second):
        top = jnp.maximum(
            jnp.max(first, axis=0, keepdims=True), jnp.max(second, axis=0, keepdims=True)
        )
        first, second = first - top, second - top
        e_first, e_second = jnp.exp2(first), jnp.exp2(second)
        total = jnp.sum(e_first, axis=0, keepdims=True) + jnp.sum(e_second, axis=0, keepdims=True)
        return first, second, e_first, e_second, total

    for h in range(heads):
        t_cols, s_cols = slice(h * dt, (h + 1) * dt), slice(h * ds, (h + 1) * ds)
        own = []
        for w in range(2):
            t_past, t_query = teacher[w][:, t_cols], teacher[w + 1][:, t_cols]
            s_past, s_query = student[w][:, s_cols], student[w + 1][:, s_cols]
            bias_past, bias_own = bias[w, :length, :], bias[w, length:, :]
            live_row = live[w]
            t0, t1, te0, te1, t_total = soft(
                scores(t_past, t_query, teacher_scale, bias_past),
                scores(t_query, t_query, teacher_scale, bias_own),
            )
            s0, s1, se0, se1, s_total = soft(
                scores(s_past, s_query, student_scale, bias_past),
                scores(s_query, s_query, student_scale, bias_own),
            )
            gap = jnp.sum(te0 * (t0 - s0), axis=0, keepdims=True) + jnp.sum(
                te1 * (t1 - s1), axis=0, keepdims=True
            )
            t_inverse = 1.0 / t_total
            divergence = gap * t_inverse * math.log(2.0) - (jnp.log(t_total) - jnp.log(s_total))
            loss[...] += divergence * live_row
            t_weight = t_inverse * (live_row * grad_scale)
            s_weight = (live_row * grad_scale) / s_total
            grad0 = (se0 * s_weight - te0 * t_weight).astype(jnp.bfloat16)
            grad1 = (se1 * s_weight - te1 * t_weight).astype(jnp.bfloat16)
            by_past = jnp.dot(grad0, s_query, preferred_element_type=jnp.float32)
            if w == 0:
                grad_past[:, s_cols] = by_past.astype(grad_past.dtype)
            else:
                own[0] = own[0] + by_past
            by_query = jnp.dot(s_past.T, grad0, preferred_element_type=jnp.float32) + jnp.dot(
                s_query.T, grad1, preferred_element_type=jnp.float32
            )
            own.append(
                by_query.T + jnp.dot(grad1, s_query, preferred_element_type=jnp.float32)
            )
        grad_first[:, s_cols] = own[0].astype(grad_first.dtype)
        grad_second[:, s_cols] = own[1]


def attention(teacher, student, bias, live):
    (length, width), ds = student[0].shape, DS // HEADS
    head_count = width // ds
    dt = teacher[0].shape[1] // head_count
    heads = min(HEADS_A_STEP, head_count)
    student_scale = 1.0 / math.sqrt(ds)
    kernel = functools.partial(
        attention_kernel, 1.0 / math.sqrt(dt), student_scale, student_scale / HEADS, heads
    )
    steps = head_count // heads
    inputs = lambda d: pl.BlockSpec((length, heads * d), lambda h: (0, h))
    columns = pl.BlockSpec((length, heads * ds), lambda h: (0, h))
    whole = lambda *shape: pl.BlockSpec(shape, lambda h: (0,) * len(shape))
    flops = 2 * head_count * length * length * (4 * dt + 4 * ds + 8 * ds)
    return pl.pallas_call(
        kernel,
        grid=(steps,),
        in_specs=[inputs(dt)] * 3
        + [inputs(ds)] * 3
        + [whole(2, 2 * length, length), whole(2, 1, length)],
        out_specs=[whole(1, length)] + [columns] * 3,
        out_shape=[
            jax.ShapeDtypeStruct((1, length), jnp.float32),
            jax.ShapeDtypeStruct((length, width), jnp.bfloat16),
            jax.ShapeDtypeStruct((length, width), jnp.bfloat16),
            jax.ShapeDtypeStruct((length, width), jnp.float32),
        ],
        compiler_params=pltpu.CompilerParams(vmem_limit_bytes=24 * 1024 * 1024),
        cost_estimate=pl.CostEstimate(
            flops=flops,
            bytes_accessed=6 * length * (dt + ds) * head_count + 8 * length * width,
            transcendentals=8 * length * length * head_count,
        ),
        name="window_attention",
    )(*teacher, *student, bias, live)


def per_device(teacher_part, student_in, out_proj, segment_ids, valid_count):
    tokens = student_in[0]
    length = tokens.shape[0]
    n_dp, n_tp, n_ctx = lax.axis_size("dp"), lax.axis_size("tp"), lax.axis_size("ctx")
    my_dp, my_tp, window = lax.axis_index("dp"), lax.axis_index("tp"), lax.axis_index("ctx")
    groups, group, place = n_ctx // 2, window >> 1, window & 1
    block_rows, width = out_proj.shape
    piece_rows, my_width = block_rows // n_dp, width // 2
    chunk_width = my_width // CHUNKS
    teacher_width = teacher_part.shape[3] // n_tp
    teacher_chunk = teacher_width // 2 // CHUNKS
    unscale = HEADS * math.sqrt(DS // HEADS)
    chunks = range(CHUNKS)

    def weight_piece(owner):
        start = (my_dp * piece_rows, owner * my_width)
        return lax.dynamic_slice(out_proj, start, (piece_rows, my_width))

    kept, sent = weight_piece(place), weight_piece(1 - place)
    swapped = swap(sent, "ctx", 1)

    pieces = split(after(tokens, kept, sent), n_ctx, n_dp)

    def piece(owner):
        return lax.dynamic_index_in_dim(pieces, owner, 0, keepdims=False)

    documents = [piece(my_dp)]
    for steps in range(1, n_dp):
        documents.append(rotate(piece(lax.rem(my_dp + steps, n_dp)), "dp", steps))
    others = [swap(rows, "ctx", 1) for rows in documents]
    pair = jnp.concatenate(ordered(kept, after(swapped, documents[-1]), place), 0)

    def teacher_columns(owner, chunk):
        starts = [
            owner * teacher_width + (half * CHUNKS + chunk) * teacher_chunk for half in range(2)
        ]
        partial = after(teacher_part, kept, sent)[0, 0]
        return [lax.dynamic_slice_in_dim(partial, start, teacher_chunk, 1) for start in starts]

    kept_columns, left_columns = [], []
    for chunk in chunks:
        total = [part.astype(jnp.float32) for part in teacher_columns(my_tp, chunk)]
        for steps in range(1, n_tp):
            leaving = jnp.concatenate(teacher_columns(lax.rem(my_tp + steps, n_tp), chunk), 1)
            arrived = rotate(after(leaving, pair) if chunk else leaving, "tp", steps)
            if chunk:
                arrived = after(arrived, kept_columns[-1], left_columns[-1])
            total = [
                t + arrived[:, half * teacher_chunk : (half + 1) * teacher_chunk].astype(jnp.float32)
                for half, t in enumerate(total)
            ]
        mine, other = ordered(*[t.astype(jnp.bfloat16) for t in total], place)
        kept_columns.append(mine)
        left_columns.append(other)

    teacher, turned = [], []
    for mine, other in zip(kept_columns, left_columns):
        if turned:
            other = after(other, turned[-1])
        turned.append(swap(other, "ctx", 1))
        teacher.append(ordered(mine, turned[-1], place))

    gates = {
        2: (others[0], left_columns[0]),
        groups - 1: (*others, left_columns[-1], turned[0]),
    }
    weights = gather_line(pair, "ctx", gates)
    rows = [jnp.concatenate(pair_of, 0) for pair_of in zip(documents, others)]
    rows_turned = row_major(jnp.concatenate(rows, 0).T)
    weights[-1] = (weights[-1][0], after(weights[-1][1], rows_turned, turned[-1]))

    def project(document):
        product = 0.0
        for source, block in weights:
            inputs = lax.dynamic_slice_in_dim(
                rows[document], source * (2 * piece_rows), 2 * piece_rows, 1
            )
            product = product + jnp.dot(inputs, block, preferred_element_type=jnp.float32)
        return product

    total = 0.0
    for steps in range(1, n_dp):
        total = total + rotate(project(steps), "dp", -steps)
    total = (project(0) + total).astype(jnp.bfloat16)
    student = ordered(total[:length], total[length:], place)

    valid = valid_count[0]
    padded = jnp.concatenate([jnp.full((length,), -1, jnp.int32), segment_ids[0]], 0)
    start = group * (2 * length)
    segments = lax.dynamic_slice_in_dim(padded, start, 3 * length, 0)
    position = start - length + jnp.arange(3 * length, dtype=jnp.int32)
    segments_kept = jnp.where(position < valid, segments, -2)
    allowed = [
        segments_kept[w * length : (w + 2) * length, None]
        == segments[None, (w + 1) * length : (w + 2) * length]
        for w in range(2)
    ]
    bias = jnp.where(jnp.stack(allowed), 0.0, MASKED).astype(jnp.float32)
    live = jnp.where(position[length:] < valid, 1.0, 0.0).astype(jnp.float32)
    live = live.reshape(2, 1, length)

    results = []
    for chunk in chunks:
        columns = slice(chunk * chunk_width, (chunk + 1) * chunk_width)
        states = [half[:, columns] for half in student]
        leaving = teacher[chunk][1]
        teacher_past = shift(after(leaving, total) if chunk else leaving, "ctx", 2)
        states = (shift(after(states[1], teacher_past), "ctx", 2), *states)
        if results:
            live = after(live, results[-1][0])
        results.append(attention((teacher_past, *teacher[chunk]), states, bias, live))

    parts, state_grad, beside = [], [], ()
    for _, grad_past, grad_first, grad_second in results:
        from_next = shift(grad_past, "ctx", -2).astype(jnp.float32)
        grad_second = (grad_second + from_next).astype(jnp.bfloat16)
        mine, other = ordered(grad_first, grad_second, place)
        block = jnp.concatenate([mine, other], 0)
        blocks = [block] + [rotate(block, "dp", steps) for steps in range(1, n_dp)]
        product = jnp.dot(
            rows_turned, jnp.concatenate(blocks, 0), preferred_element_type=jnp.float32
        )
        total, beside = scatter_line(product.reshape(groups, 2 * piece_rows, chunk_width), "ctx")
        state_grad.append(ordered(mine, swap(after(other, blocks[-1]), "ctx", 1), place))

        total = total.astype(jnp.bfloat16)
        mine = lax.dynamic_slice_in_dim(total, place * piece_rows, piece_rows, 0)
        other = lax.dynamic_slice_in_dim(total, (1 - place) * piece_rows, piece_rows, 0)
        total = jnp.concatenate(ordered(mine, swap(other, "ctx", 1), place), 1)
        owners = [total] + [rotate(total, "dp", steps) for steps in range(1, n_dp)]
        parts.append(jnp.concatenate(by_owner(owners, my_dp), 0))

    halves = [slice(half * chunk_width, (half + 1) * chunk_width) for half in range(2)]
    wo_grad = jnp.concatenate([part[:, half] for half in halves for part in parts], 1)
    state_grad = jnp.concatenate([pair[half] for half in range(2) for pair in state_grad], 1)
    state_grad = state_grad.astype(jnp.float32) * unscale

    doc_loss = sum(jnp.sum(loss) for loss, *_ in results) / HEADS
    doc_loss = jnp.broadcast_to(doc_loss, (1, 128))
    steps = [("tp", 1 << bit) for bit in range(n_tp.bit_length() - 1)]
    steps += [("ctx", 1 << bit) for bit in range(n_ctx.bit_length() - 1)]
    for axis, distance in steps:
        if axis == "ctx" and distance > 1:
            doc_loss = after(doc_loss, *beside)
        doc_loss = doc_loss + swap(doc_loss, axis, distance)
    return (doc_loss[0, :1], wo_grad.astype(jnp.float32), state_grad[None])


def solution(mesh):
    return jax.shard_map(
        per_device,
        mesh=mesh,
        in_specs=(
            P("dp", "tp", "ctx", None),
            P("dp", "ctx", None),
            P("ctx", "tp"),
            P("dp", None),
            P("dp"),
        ),
        out_specs=(P("dp"), P("ctx", "tp"), P("dp", "ctx", "tp")),
        check_vma=False,
    )
```

```python
import functools
import math

import jax
import jax.numpy as jnp
from jax import lax
from jax.experimental import pallas as pl
from jax.experimental.layout import Layout, with_layout_constraint
from jax.experimental.pallas import tpu as pltpu
from jax.sharding import PartitionSpec as P

DS = 4096
HEADS = 32
CHUNKS = 2
HEADS_A_STEP = 2
MASKED = -1e30


def after(value, *earlier):
    return lax.optimization_barrier((value, *earlier))[0]


def row_major(value):
    return with_layout_constraint(value, Layout(tuple(range(value.ndim))))


def rotate(value, axis, steps):
    count = lax.axis_size(axis)
    return lax.ppermute(value, axis, [(i, (i + steps) % count) for i in range(count)])


def swap(value, axis, distance):
    count = lax.axis_size(axis)
    return lax.ppermute(value, axis, [(i, i ^ distance) for i in range(count)])


def shift(value, axis, steps):
    count = lax.axis_size(axis)
    pairs = [(i, i + steps) for i in range(count) if 0 <= i + steps < count]
    return lax.ppermute(value, axis, pairs)


def ordered(mine, other, place):
    first = lax.select(place == 0, mine, other)
    second = lax.select(place == 0, other, mine)
    return first, second


def send_line(value, axis, upward=(), downward=()):
    pairs = [(2 * i + j, 2 * i + 2 + j) for i in upward for j in range(2)]
    pairs += [(2 * i + j, 2 * i - 2 + j) for i in downward for j in range(2)]
    return lax.ppermute(value, axis, pairs)


def to_neighbours(value, axis):
    groups = lax.axis_size(axis) // 2
    return (
        send_line(value, axis, upward=range(groups - 1)),
        send_line(value, axis, downward=range(1, groups)),
    )


def gather_line(block, axis, gates, neighbours):
    groups, group = lax.axis_size(axis) // 2, lax.axis_index(axis) >> 1
    (up, down), out, either = neighbours, [(group, block)], None
    for hop in range(1, groups):
        upward, downward = range(hop - 1, groups - 1), range(1, groups - hop + 1)
        gate = gates.get(hop, ())
        below, above = jnp.maximum(group - hop, 0), jnp.minimum(group + hop, groups - 1)
        if either is None:
            if hop > 1:
                if gate:
                    up, down = after(up, *gate), after(down, *gate)
                up = send_line(up, axis, upward=upward)
                down = send_line(down, axis, downward=downward)
            if 2 * hop < groups:
                out += [(below, up), (above, down)]
                continue
            either = lax.select(group >= hop, up, down)
        else:
            if gate:
                either = after(either, *gate)
            either = send_line(either, axis, upward, downward)
        out.append((lax.select(group >= hop, below, above), either))
    return out


def scatter_line(blocks, axis):
    groups, group = lax.axis_size(axis) // 2, lax.axis_index(axis) >> 1

    def plus(target, came):
        block = lax.dynamic_index_in_dim(blocks, target, 0, keepdims=False)
        return block if came is None else block + came.astype(jnp.float32)

    up = down = None
    for step in range(1, groups):
        upward, downward = range(min(step, groups - 1)), range(max(groups - step, 1), groups)
        rising = plus(jnp.minimum(groups - step + group, groups - 1), up).astype(jnp.bfloat16)
        falling = plus(jnp.maximum(group + step - groups, 0), down).astype(jnp.bfloat16)
        if 2 * step < groups - 1:
            value = lax.select(group < step, rising, falling)
            came = send_line(value, axis, upward, downward)
            none = jnp.zeros_like(came)
            up = lax.select(group <= step, came, none)
            down = lax.select(group >= groups - 1 - step, came, none)
        else:
            up = send_line(rising, axis, upward=upward)
            down = send_line(falling, axis, downward=downward)
    return plus(group, up) + down.astype(jnp.float32), (up, down)


def by_owner(parts, me):
    count = len(parts)
    if count == 2:
        return ordered(*parts, me)
    parts = jnp.stack(parts)
    return [
        lax.dynamic_index_in_dim(parts, lax.rem(me + count - i, count), 0, keepdims=False)
        for i in range(count)
    ]


def split_kernel(count, rows, tokens, out):
    width = tokens.shape[1] // count // rows
    for piece in range(count):
        for row in range(rows):
            start = (row * count + piece) * width
            out[piece, :, row * width : (row + 1) * width] = tokens[:, start : start + width]


def split(tokens, blocks, count):
    length, width = tokens.shape
    rows = max(1, 128 * blocks * count // width)
    step = width // blocks * rows
    return pl.pallas_call(
        functools.partial(split_kernel, count, rows),
        grid=(blocks // rows,),
        in_specs=[pl.BlockSpec((length, step), lambda i: (0, i))],
        out_specs=pl.BlockSpec((count, length, step // count), lambda i: (0, 0, i)),
        out_shape=jax.ShapeDtypeStruct((count, length, width // count), tokens.dtype),
        compiler_params=pltpu.CompilerParams(vmem_limit_bytes=16 * 1024 * 1024),
        cost_estimate=pl.CostEstimate(
            flops=0, bytes_accessed=4 * length * width, transcendentals=0
        ),
        name="split_tokens",
    )(tokens)


def turn_kernel(place, mine, other, out):
    length = mine.shape[0]
    out[:length, :] = mine[...]
    out[length:, :] = other[...]


def turn(mine, other, place, blocks):
    length, width = mine.shape
    step = width // blocks
    columns = pl.BlockSpec((length, step), lambda i, place: (0, i ^ place[0]))
    if step % 128:
        both = jnp.concatenate([mine, other], 0)
        pieces = [
            lax.dynamic_slice_in_dim(both, (i ^ place) * step, step, 1) for i in range(blocks)
        ]
        return jnp.concatenate(pieces, 1)
    return pl.pallas_call(
        turn_kernel,
        grid_spec=pltpu.PrefetchScalarGridSpec(
            num_scalar_prefetch=1,
            grid=(blocks,),
            in_specs=[columns, columns],
            out_specs=pl.BlockSpec((2 * length, step), lambda i, place: (0, i)),
        ),
        out_shape=jax.ShapeDtypeStruct((2 * length, width), mine.dtype),
        compiler_params=pltpu.CompilerParams(vmem_limit_bytes=16 * 1024 * 1024),
        cost_estimate=pl.CostEstimate(
            flops=0, bytes_accessed=12 * length * width, transcendentals=0
        ),
        name="turn_tokens",
    )(place.reshape(1).astype(jnp.int32), mine, other)


def attention_kernel(teacher_scale, student_scale, grad_scale, heads, *refs):
    teacher, student = refs[0:3], refs[3:6]
    bias, live, loss = refs[6], refs[7], refs[8]
    grad_past, grad_first, grad_second = refs[9:12]
    length = student[0].shape[0]
    dt, ds = teacher[0].shape[1] // heads, student[0].shape[1] // heads
    log2e = math.log2(math.e)

    @pl.when(pl.program_id(0) == 0)
    def _():
        loss[...] = jnp.zeros_like(loss)

    def scores(keys, queries, scale, mask):
        product = lax.dot_general(
            keys, queries, (((1,), (1,)), ((), ())), preferred_element_type=jnp.float32
        )
        return product * (scale * log2e) + mask

    def soft(first, second):
        top = jnp.maximum(
            jnp.max(first, axis=0, keepdims=True), jnp.max(second, axis=0, keepdims=True)
        )
        first, second = first - top, second - top
        e_first, e_second = jnp.exp2(first), jnp.exp2(second)
        total = jnp.sum(e_first, axis=0, keepdims=True) + jnp.sum(e_second, axis=0, keepdims=True)
        return first, second, e_first, e_second, total

    for h in range(heads):
        t_cols, s_cols = slice(h * dt, (h + 1) * dt), slice(h * ds, (h + 1) * ds)
        own = []
        for w in range(2):
            t_past, t_query = teacher[w][:, t_cols], teacher[w + 1][:, t_cols]
            s_past, s_query = student[w][:, s_cols], student[w + 1][:, s_cols]
            bias_past, bias_own = bias[w, :length, :], bias[w, length:, :]
            live_row = live[w]
            t0, t1, te0, te1, t_total = soft(
                scores(t_past, t_query, teacher_scale, bias_past),
                scores(t_query, t_query, teacher_scale, bias_own),
            )
            s0, s1, se0, se1, s_total = soft(
                scores(s_past, s_query, student_scale, bias_past),
                scores(s_query, s_query, student_scale, bias_own),
            )
            gap = jnp.sum(te0 * (t0 - s0), axis=0, keepdims=True) + jnp.sum(
                te1 * (t1 - s1), axis=0, keepdims=True
            )
            t_inverse = 1.0 / t_total
            divergence = gap * t_inverse * math.log(2.0) - (jnp.log(t_total) - jnp.log(s_total))
            loss[...] += divergence * live_row
            t_weight = t_inverse * (live_row * grad_scale)
            s_weight = (live_row * grad_scale) / s_total
            grad0 = (se0 * s_weight - te0 * t_weight).astype(jnp.bfloat16)
            grad1 = (se1 * s_weight - te1 * t_weight).astype(jnp.bfloat16)
            by_past = jnp.dot(grad0, s_query, preferred_element_type=jnp.float32)
            if w == 0:
                grad_past[:, s_cols] = by_past.astype(grad_past.dtype)
            else:
                own[0] = own[0] + by_past
            by_query = jnp.dot(s_past.T, grad0, preferred_element_type=jnp.float32) + jnp.dot(
                s_query.T, grad1, preferred_element_type=jnp.float32
            )
            own.append(
                by_query.T + jnp.dot(grad1, s_query, preferred_element_type=jnp.float32)
            )
        grad_first[:, s_cols] = own[0].astype(grad_first.dtype)
        grad_second[:, s_cols] = own[1]


def attention(teacher, student, bias, live, chunk):
    length, ds = student[0].shape[0], DS // HEADS
    width = student[0].shape[1] // CHUNKS
    head_count = width // ds
    dt = teacher[0].shape[1] // CHUNKS // head_count
    heads = min(HEADS_A_STEP, head_count)
    student_scale = 1.0 / math.sqrt(ds)
    kernel = functools.partial(
        attention_kernel, 1.0 / math.sqrt(dt), student_scale, student_scale / HEADS, heads
    )
    steps = head_count // heads
    inputs = lambda d: pl.BlockSpec((length, heads * d), lambda h: (0, h + chunk * steps))
    columns = pl.BlockSpec((length, heads * ds), lambda h: (0, h))
    whole = lambda *shape: pl.BlockSpec(shape, lambda h: (0,) * len(shape))
    return pl.pallas_call(
        kernel,
        grid=(steps,),
        in_specs=[inputs(dt)] * 3
        + [inputs(ds)] * 3
        + [whole(2, 2 * length, length), whole(2, 1, length)],
        out_specs=[whole(1, length)] + [columns] * 3,
        out_shape=[
            jax.ShapeDtypeStruct((1, length), jnp.float32),
            jax.ShapeDtypeStruct((length, width), jnp.bfloat16),
            jax.ShapeDtypeStruct((length, width), jnp.bfloat16),
            jax.ShapeDtypeStruct((length, width), jnp.float32),
        ],
        compiler_params=pltpu.CompilerParams(vmem_limit_bytes=24 * 1024 * 1024),
        cost_estimate=pl.CostEstimate(
            flops=2 * head_count * length * length * (4 * dt + 12 * ds),
            bytes_accessed=6 * length * (dt + ds) * head_count + 8 * length * width,
            transcendentals=8 * length * length * head_count,
        ),
        name="window_attention",
    )(*teacher, *student, bias, live)


def per_device(teacher_part, student_in, out_proj, segment_ids, valid_count):
    tokens = student_in[0]
    length = tokens.shape[0]
    n_dp, n_tp, n_ctx = lax.axis_size("dp"), lax.axis_size("tp"), lax.axis_size("ctx")
    my_dp, my_tp, window = lax.axis_index("dp"), lax.axis_index("tp"), lax.axis_index("ctx")
    groups, group, place = n_ctx // 2, window >> 1, window & 1
    block_rows, width = out_proj.shape
    piece_rows, my_width = block_rows // n_dp, width // 2
    chunk_width = my_width // CHUNKS
    teacher_width = teacher_part.shape[3] // n_tp
    unscale = HEADS * math.sqrt(DS // HEADS)
    chunks = range(CHUNKS)

    def weight_piece(owner):
        start = (my_dp * piece_rows, owner * my_width)
        return lax.dynamic_slice(out_proj, start, (piece_rows, my_width))

    kept, sent = weight_piece(place), weight_piece(1 - place)
    own_rows = to_neighbours(kept, "ctx")
    swapped = swap(sent, "ctx", 1)
    pair_rows = to_neighbours(after(swapped, *own_rows), "ctx")
    neighbours = [jnp.concatenate(halves, 0) for halves in zip(own_rows, pair_rows)]

    pieces = split(after(tokens, kept, sent), n_ctx, n_dp)

    def piece(owner):
        return lax.dynamic_index_in_dim(pieces, owner, 0, keepdims=False)

    documents = [piece(my_dp)]
    for steps in range(1, n_dp):
        documents.append(rotate(piece(lax.rem(my_dp + steps, n_dp)), "dp", steps))
    others = [swap(rows, "ctx", 1) for rows in documents]

    def teacher_columns(owner):
        return lax.dynamic_slice_in_dim(
            after(teacher_part, kept, sent)[0, 0], owner * teacher_width, teacher_width, 1
        )

    total = teacher_columns(my_tp).astype(jnp.float32)
    for steps in range(1, n_tp):
        received = rotate(teacher_columns(lax.rem(my_tp + steps, n_tp)), "tp", steps)
        total = total + received.astype(jnp.float32)
    total = total.astype(jnp.bfloat16)
    mine = lax.dynamic_slice_in_dim(total, place * (teacher_width // 2), teacher_width // 2, 1)
    other = lax.dynamic_slice_in_dim(
        total, (1 - place) * (teacher_width // 2), teacher_width // 2, 1
    )
    turned = swap(after(other, others[-1]), "ctx", 1)
    teacher = ordered(mine, turned, place)
    teacher = (shift(teacher[1], "ctx", 2), *teacher)

    gates = {groups - 1: (others[0], other)}
    weights = gather_line(jnp.concatenate([kept, swapped], 0), "ctx", gates, neighbours)
    rows = [turn(mine, other, place, n_ctx) for mine, other in zip(documents, others)]
    rows_turned = row_major(jnp.concatenate(rows, 0).T)

    def product_of(document, source, block):
        inputs = lax.dynamic_slice_in_dim(
            rows[document], source * (2 * piece_rows), 2 * piece_rows, 1
        )
        return jnp.dot(inputs, block, preferred_element_type=jnp.float32)

    early = [
        sum(product_of(document, *weight) for weight in weights[:-1]) for document in range(n_dp)
    ]
    source, block = weights[-1]
    block = after(block, *early, teacher[1], rows_turned)
    total = 0.0
    for steps in range(1, n_dp):
        total = total + rotate(early[steps] + product_of(steps, source, block), "dp", -steps)
    total = (early[0] + product_of(0, source, block) + total).astype(jnp.bfloat16)
    student = ordered(total[:length], total[length:], place)
    student = (shift(student[1], "ctx", 2), *student)

    valid = valid_count[0]
    padded = jnp.concatenate([jnp.full((length,), -1, jnp.int32), segment_ids[0]], 0)
    start = group * (2 * length)
    segments = lax.dynamic_slice_in_dim(padded, start, 3 * length, 0)
    position = start - length + jnp.arange(3 * length, dtype=jnp.int32)
    segments_kept = jnp.where(position < valid, segments, -2)
    allowed = [
        segments_kept[w * length : (w + 2) * length, None]
        == segments[None, (w + 1) * length : (w + 2) * length]
        for w in range(2)
    ]
    bias = jnp.where(jnp.stack(allowed), 0.0, MASKED).astype(jnp.float32)
    live = jnp.where(position[length:] < valid, 1.0, 0.0).astype(jnp.float32)
    live = live.reshape(2, 1, length)

    results = []
    for chunk in chunks:
        if chunk:
            live = after(live, results[-1][0])
        results.append(attention(teacher, student, bias, live, chunk))

    parts, state_grad, beside = [], [], ()
    for _, grad_past, grad_first, grad_second in results:
        from_next = shift(grad_past, "ctx", -2)
        from_next = from_next.astype(jnp.float32)
        grad_second = (grad_second + from_next).astype(jnp.bfloat16)
        mine, other = ordered(grad_first, grad_second, place)
        block = jnp.concatenate([mine, other], 0)
        blocks = [block] + [rotate(block, "dp", steps) for steps in range(1, n_dp)]
        product = jnp.dot(
            rows_turned, jnp.concatenate(blocks, 0), preferred_element_type=jnp.float32
        )
        total, beside = scatter_line(product.reshape(groups, 2 * piece_rows, chunk_width), "ctx")
        state_grad.append(ordered(mine, swap(after(other, blocks[-1]), "ctx", 1), place))

        total = total.astype(jnp.bfloat16)
        mine, other = total[:piece_rows], total[piece_rows:]
        total = jnp.concatenate(ordered(mine, swap(other, "ctx", 1), place), 1)
        owners = [total] + [rotate(total, "dp", steps) for steps in range(1, n_dp)]
        parts.append(jnp.concatenate(by_owner(owners, my_dp), 0))

    halves = [slice(half * chunk_width, (half + 1) * chunk_width) for half in range(2)]
    wo_grad = jnp.concatenate([part[:, half] for half in halves for part in parts], 1)
    state_grad = jnp.concatenate([pair[half] for half in range(2) for pair in state_grad], 1)
    state_grad = state_grad.astype(jnp.float32) * unscale

    doc_loss = sum(jnp.sum(loss) for loss, *_ in results) / HEADS
    doc_loss = jnp.broadcast_to(doc_loss, (1, 128))
    steps = [("tp", 1 << bit) for bit in range(n_tp.bit_length() - 1)]
    steps += [("ctx", 1 << bit) for bit in range(n_ctx.bit_length() - 1)]
    for axis, distance in steps:
        if axis == "ctx" and distance > 1:
            doc_loss = after(doc_loss, *beside)
        doc_loss = doc_loss + swap(doc_loss, axis, distance)
    return (doc_loss[0, :1], wo_grad.astype(jnp.float32), state_grad[None])


def solution(mesh):
    return jax.shard_map(
        per_device,
        mesh=mesh,
        in_specs=(
            P("dp", "tp", "ctx", None),
            P("dp", "ctx", None),
            P("ctx", "tp"),
            P("dp", None),
            P("dp"),
        ),
        out_specs=(P("dp"), P("ctx", "tp"), P("dp", "ctx", "tp")),
        check_vma=False,
    )
```
